32 devices in a mesh: grp: 2 (over y), db: 4 (over z), head: 2 (over x), sub: 2 (over core).
Axes of the slice: x: 2, y: 2, z: 4, core: 2. Of those that a mesh axis runs over, the one named last changes fastest.
Arguments:
- activations: bfloat16 [512, 8192], P(('grp', 'head', 'sub'), 'db'), parts along dimension 0, may hold values from -24 to 24
- w_query: bfloat16 [8192, 4096], P('db', ('head', 'sub')), may hold values from -0.0625 to 0.0625
- w_out: bfloat16 [4096, 8192], P(('head', 'sub'), 'db'), may hold values from -0.09375 to 0.09375
- w_up: bfloat16 [8192, 16384], P('db', ('head', 'sub')), may hold values from -0.0625 to 0.0625
- w_down: bfloat16 [16384, 8192], P(('head', 'sub'), 'db'), may hold values from -0.09375 to 0.09375
- kv_store: bfloat16 [64, 2, 128, 4096], P(('grp', 'db'), None, None, ('head', 'sub')), parts along dimension 0, may hold values from -330 to 330
- neighbours: int32 [8, 2], P('grp'), parts along dimension 0, may hold values from 0 to 31, as said below
- block_place: int32 [64], P('grp'), parts along dimension 0, may hold values from 0 to 31, as said below
Outputs:
- layer_out: bfloat16 [512, 8192], P(('grp', 'head', 'sub'), 'db'), parts along dimension 0
The draws below stay inside these ranges and needn't reach their ends.
There are 2 independent parts, one for each index of `grp`. The reference program is written for one: setup_inputs(seed, part) draws one part's arguments, and reference() takes and returns one part's arrays. A program takes and returns all parts, laid end to end along the dimension named above; an argument that names none is the same for every part. Nothing has to cross between parts.
Inputs may be any that keep to these rules, and one draw needn't show every extreme that they name: `neighbours`: the 2 blocks named by a span and the 2 blocks named by the span before it lie on 4 different shards, the shard of block b being block_place[b] // 8. Each store position appears once; block b is kept at position block_place[b] of kv_store.
All inputs are finite; a program needn't handle non-finite values.
Results may differ from the reference program's by a relative error of at most 0.017.
Values may be sent and summed in bfloat16 or wider, within the bound.
A program may use at most 128 MiB of HBM per device.

```python
import jax
import jax.numpy as jnp
from jax import lax

D = 8192
HEADS = 32
HDIM = 128
FF = 16384
SPAN = 64
NEIGH = 2
NTOK = 128
BLK_DEV = 8
SPANS = 4
ROWS = 256
NBLK = 32
N_DB = 4
N_HEAD = 2
N_SUB = 2


def layout(key):
    block_pos = jax.random.permutation(jax.random.fold_in(key, 11), NBLK).astype(jnp.int32)
    heat_level = jax.random.randint(jax.random.fold_in(key, 12), (N_DB,), 1, 9, dtype=jnp.int32)
    score_bits = jax.random.randint(jax.random.fold_in(key, 13), (SPANS, N_DB), 0, 4096, dtype=jnp.int32)
    slot_draw = jax.random.randint(jax.random.fold_in(key, 14), (SPANS, NEIGH), 0, BLK_DEV, dtype=jnp.int32)
    shards = jnp.arange(N_DB, dtype=jnp.int32)

    def choose_owners(before, scores):
        ranking = scores * heat_level * N_DB + shards
        banned = jnp.any(shards[:, None] == before[None, :], axis=1)
        ranking = jnp.where(banned, -1, ranking)
        chosen = lax.top_k(ranking, NEIGH)[1].astype(jnp.int32)
        return (chosen, chosen)
    initial = jnp.full((NEIGH,), -1, jnp.int32)
    owners = lax.scan(choose_owners, initial, score_bits)[1]
    holder = jnp.argsort(block_pos, stable=True).astype(jnp.int32)
    picked = jnp.take(holder, (owners * BLK_DEV + slot_draw).reshape(-1), axis=0).reshape(SPANS, NEIGH)
    return (block_pos, picked.astype(jnp.int32))


def draw_block_place(key, part):
    block_pos, picked = layout(key)
    return block_pos


def draw_neighbours(key, part):
    block_pos, picked = layout(key)
    return picked


def draw_activations(key, part):
    key = jax.random.fold_in(key, 1)
    row_scale = jnp.exp(jax.random.uniform(jax.random.fold_in(key, 1), (ROWS, 1), jnp.float32, jnp.log(0.1), jnp.log(1.0)))
    position = jnp.arange(D, dtype=jnp.float32) / D - 0.5
    col_rise = jnp.exp(jnp.log(10.0) * position)[None, :]
    col_scale = col_rise * jnp.exp(jax.random.uniform(jax.random.fold_in(key, 2), (1, D), jnp.float32, jnp.log(0.55), jnp.log(1.8)))
    base_draw = jnp.clip(jax.random.normal(jax.random.fold_in(key, 3), (ROWS, D), jnp.float32), -4.0, 4.0)
    return (base_draw * row_scale * col_scale).astype(jnp.bfloat16)


def draw_kv_store(key, part):
    key = jax.random.fold_in(key, 2)
    shape_one = (NBLK, 1, NTOK, HEADS * HDIM)
    key_part = jnp.clip(jax.random.normal(jax.random.fold_in(key, 1), shape_one, jnp.float32), -5.0, 5.0)
    value_part = jnp.clip(jax.random.normal(jax.random.fold_in(key, 2), shape_one, jnp.float32), -5.0, 5.0)
    return jnp.concatenate([key_part, value_part], 1).astype(jnp.bfloat16)


def block_levels(key, dims, cuts, smallest, largest):
    def one(axis_at, parts):
        draws = jax.random.uniform(jax.random.fold_in(jax.random.fold_in(key, 6), axis_at), (parts,), jnp.float32, smallest / len(cuts), largest / len(cuts))
        return jnp.repeat(jnp.exp(draws), dims[axis_at] // parts).reshape((-1,) + (1,) * (len(dims) - axis_at - 1))

    factor_of = one(*cuts[0])
    for cut in cuts[1:]:
        factor_of = factor_of * one(*cut)
    return factor_of


def scatter_about(stream_key, dims, width, most, cuts=(), kind=jnp.bfloat16):
    loudness = block_levels(stream_key, dims, cuts, -0.22, 0.18) if cuts else 1.0
    entries = jax.random.normal(stream_key, dims, jnp.float32) * width * loudness
    return jnp.minimum(jnp.maximum(entries, -most), most).astype(kind)


def setup_inputs(seed: int = 0, part: int = 0) -> dict:
    arg_keys = jax.random.split(jax.random.key(seed), 9)
    part_splits = jax.random.split(jax.random.fold_in(arg_keys[8], part), 9)
    return {
        "activations": draw_activations(jax.random.fold_in(jax.random.fold_in(arg_keys[8], part), 71), part),
        "w_query": scatter_about(arg_keys[1], (D, HEADS * HDIM), D ** -0.5, 0.0625, ((0, 4), (1, 4))),
        "w_out": scatter_about(arg_keys[2], (HEADS * HDIM, D), (HEADS * HDIM) ** -0.5, 0.09375, ((0, 4), (1, 4))),
        "w_up": scatter_about(arg_keys[3], (D, FF), D ** -0.5, 0.0625, ((0, 4), (1, 4))),
        "w_down": scatter_about(arg_keys[4], (FF, D), (FF // 4) ** -0.5, 0.09375, ((0, 4), (1, 4))),
        "kv_store": draw_kv_store(jax.random.fold_in(jax.random.fold_in(arg_keys[8], part), 71), part),
        "neighbours": draw_neighbours(jax.random.fold_in(jax.random.fold_in(arg_keys[8], part), 71), part),
        "block_place": draw_block_place(jax.random.fold_in(jax.random.fold_in(arg_keys[8], part), 71), part),
    }


def normalize(values):
    row_total = lax.optimization_barrier(jnp.sum(values, axis=1, keepdims=True))
    squares = lax.optimization_barrier(jnp.sum(values * values, axis=1, keepdims=True))
    row_mean = row_total / D
    row_var = squares / D - row_mean * row_mean
    return ((values - row_mean) * lax.rsqrt(row_var + 1e-05)).astype(jnp.bfloat16)

def block_sum(left_side, right_side, pieces):
    block_width = left_side.shape[1] // pieces

    def add_block(running, block_index):
        part_left = lax.dynamic_slice_in_dim(left_side, block_index * block_width, block_width, 1)
        part_right = lax.dynamic_slice_in_dim(right_side, block_index * block_width, block_width, 0)
        partial_term = jnp.dot(part_left, part_right, preferred_element_type=jnp.float32).astype(jnp.bfloat16)
        partial_term = lax.optimization_barrier(partial_term)
        return (running + partial_term.astype(jnp.float32), None)
    initial = jnp.zeros((left_side.shape[0], right_side.shape[1]), jnp.float32)
    return lax.scan(add_block, initial, jnp.arange(pieces, dtype=jnp.int32))[0]

def reference(activations, w_query, w_out, w_up, w_down, kv_store, neighbours, block_place):
    inputs = activations.astype(jnp.float32)
    normed = normalize(inputs)
    queries = jnp.dot(normed, w_query, preferred_element_type=jnp.float32).astype(jnp.bfloat16)
    full_width = HEADS * HDIM
    shifted = jnp.concatenate([queries[SPAN - 1:], jnp.zeros((SPAN - 1, full_width), jnp.bfloat16)], 0)
    grouped = shifted.reshape(SPANS, SPAN, HEADS, HDIM).astype(jnp.float32)
    where_at = jnp.take(block_place, neighbours.reshape(-1), axis=0).astype(jnp.int32)
    fetched = jnp.take(kv_store, where_at, axis=0).reshape(SPANS, NEIGH, 2, NTOK, HEADS, HDIM)
    keys_all = fetched[:, :, 0].reshape(SPANS, NEIGH * NTOK, HEADS, HDIM).astype(jnp.float32)
    values_all = fetched[:, :, 1].reshape(SPANS, NEIGH * NTOK, HEADS, HDIM).astype(jnp.float32)
    scores = jnp.einsum('crhe,ckhe->chrk', grouped, keys_all) * HDIM ** (-0.5)
    top_score = lax.optimization_barrier(jnp.max(scores, axis=-1, keepdims=True))
    exponent = jnp.exp(scores - top_score)
    weights = (exponent / lax.optimization_barrier(jnp.sum(exponent, axis=-1, keepdims=True))).astype(jnp.bfloat16)
    heads_out = jnp.einsum('chrk,ckhe->crhe', weights.astype(jnp.float32), values_all).astype(jnp.bfloat16)
    flat_out = heads_out.reshape(ROWS, full_width)
    attended = jnp.concatenate([jnp.zeros((SPAN - 1, full_width), jnp.bfloat16), flat_out[:ROWS - SPAN + 1]], 0)
    state_rows = inputs + jnp.dot(attended, w_out, preferred_element_type=jnp.float32)
    normed_mid = normalize(state_rows)
    lifted = block_sum(normed_mid, w_up, N_DB)
    activated = jax.nn.gelu(lifted, approximate=True).astype(jnp.bfloat16)
    lowered = block_sum(activated, w_down, N_HEAD * N_SUB)
    return (state_rows + lowered).astype(jnp.bfloat16)
```

```python
import jax
import jax.numpy as jnp
from jax import lax
from jax.experimental import pallas as pl
from jax.experimental.pallas import tpu as pltpu
from jax.sharding import PartitionSpec as P

D = 8192
HDIM = 128
NEIGH = 2
NTOK = 128
VMEM_BYTES = 63 * 1024 * 1024


def apply_norm(values, row_sums):
    row_mean = row_sums[0] / D
    row_var = row_sums[1] / D - row_mean * row_mean
    return ((values - row_mean) * lax.rsqrt(row_var + 1e-05)).astype(jnp.bfloat16)


def local(activations, w_query, w_out, w_up, w_down, kv_store, neighbours, block_place):
    shards = lax.axis_size("db")
    my_index = lax.axis_index("db")
    inputs = lax.all_gather(activations, ("head", "sub"), axis=0, tiled=True).astype(jnp.float32)
    sums_in = lax.psum(
        (jnp.sum(inputs, axis=1, keepdims=True), jnp.sum(inputs * inputs, axis=1, keepdims=True)),
        "db",
    )
    normed = apply_norm(inputs, sums_in)
    queries = lax.psum_scatter(
        jnp.dot(normed, w_query, preferred_element_type=jnp.float32),
        "db",
        scatter_dimension=0,
        tiled=True,
    ).astype(jnp.bfloat16)
    local_width = queries.shape[1]
    head_count = local_width // HDIM
    span_rows = queries.shape[0]
    earlier = lax.dynamic_slice_in_dim(neighbours, jnp.maximum(my_index - 1, 0), 1, 0)
    current = lax.dynamic_slice_in_dim(neighbours, my_index, 1, 0)
    wanted = jnp.concatenate([earlier, current], 0).reshape(-1)
    block_ids = jnp.arange(block_place.shape[0], dtype=jnp.int32)
    located = jnp.sum(
        jnp.where(block_ids[None, :] == wanted[:, None], block_place[None, :], 0), axis=1
    )
    store_blocks = kv_store.shape[0]
    owner_of = located // store_blocks
    slot_of = located % store_blocks
    request_ids = jnp.arange(2 * NEIGH, dtype=jnp.int32)
    segment_of = (request_ids >= NEIGH).astype(jnp.int32)
    usable = jnp.where(request_ids < NEIGH, my_index > 0, True)
    peer_ids = jnp.arange(shards, dtype=jnp.int32)
    coded_slot = 2 * slot_of + segment_of + 1
    request_out = (
        jnp.sum(
            jnp.where(
                (owner_of[None, :] == peer_ids[:, None]) & usable[None, :], coded_slot[None, :], 0
            ),
            axis=1,
            keepdims=True,
        )
        - 1
    )
    request_in = lax.all_to_all(request_out, "db", split_axis=0, concat_axis=0, tiled=True)
    asked_for = request_in[:, 0]
    chosen_slot = jnp.maximum(asked_for, 0) // 2
    row_index = jnp.arange(span_rows, dtype=jnp.int32)
    row_segment = (row_index == span_rows - 1).astype(jnp.int32)
    row_live = (row_index == span_rows - 1) | (my_index > 0)
    score_scale = HDIM ** (-0.5)
    outgoing = jnp.take(kv_store, chosen_slot, axis=0)
    outgoing = jnp.where((asked_for >= 0)[:, None, None, None], outgoing, jnp.zeros_like(outgoing))
    arrived = lax.all_to_all(outgoing, "db", split_axis=0, concat_axis=0, tiled=True)
    needed = jnp.take(arrived, owner_of, axis=0)
    key_block = needed[:, 0].reshape(-1, head_count, HDIM)
    value_block = needed[:, 1].reshape(-1, head_count, HDIM)
    query_heads = queries.reshape(span_rows, head_count, HDIM)
    scores = (
        jnp.einsum("rhe,khe->hrk", query_heads, key_block, preferred_element_type=jnp.float32)
        * score_scale
    )
    key_request = jnp.arange(key_block.shape[0], dtype=jnp.int32) // NTOK
    key_live = (segment_of[key_request][None, :] == row_segment[:, None]) & usable[key_request][
        None, :
    ]
    scores = jnp.where(key_live[None], scores, -1e30)
    top_score = jnp.max(scores, axis=-1, keepdims=True)
    exponent = jnp.exp(scores - top_score)
    weights = (exponent / jnp.sum(exponent, axis=-1, keepdims=True)).astype(jnp.bfloat16)
    attended = jnp.einsum("hrk,khe->rhe", weights, value_block, preferred_element_type=jnp.float32)
    attended = attended.reshape(span_rows, local_width).astype(jnp.bfloat16)
    attended = jnp.where(row_live[:, None], attended, jnp.zeros_like(attended))
    attn_part = jnp.dot(
        lax.all_gather(attended, "db", axis=0, tiled=True),
        w_out,
        preferred_element_type=jnp.float32,
    )
    attn_full = lax.psum(attn_part, ("head", "sub"))
    state_rows = inputs + attn_full
    sums_mid = lax.psum(
        (
            jnp.sum(state_rows, axis=1, keepdims=True),
            jnp.sum(state_rows * state_rows, axis=1, keepdims=True),
        ),
        "db",
    )
    normed_mid = apply_norm(state_rows, sums_mid)
    lifted = lax.psum_scatter(
        jnp.dot(normed_mid, w_up, preferred_element_type=jnp.float32).astype(jnp.bfloat16),
        "db",
        scatter_dimension=0,
        tiled=True,
    ).astype(jnp.float32)
    activated = jax.nn.gelu(lifted, approximate=True).astype(jnp.bfloat16)
    gathered = lax.all_gather(activated, "db", axis=0, tiled=True)
    group_rows = state_rows.shape[0] // lax.axis_size(("head", "sub"))
    lowered = lax.psum_scatter(
        jnp.dot(gathered, w_down, preferred_element_type=jnp.float32).astype(jnp.bfloat16),
        ("head", "sub"),
        scatter_dimension=0,
        tiled=True,
    ).astype(jnp.float32)
    own_state = lax.dynamic_slice_in_dim(
        state_rows, lax.axis_index(("head", "sub")) * group_rows, group_rows, 0
    )
    return (own_state + lowered).astype(jnp.bfloat16)


def dot(left, right):
    return jnp.dot(left, right, preferred_element_type=jnp.float32)


def layer_kernel(
    act, wq_hbm, wo_hbm, wu_hbm, wd_hbm, kv_hbm, near, place, out,
    wq, wu, wd, kvs, xg, st_in, st_tot, nx, qp, qr, qg, ob, lse, att,
    op, orx, state, st_mid, ng, lp, lr, ag, acc, dp, dr,
    local_sem, wd0_sem, x_s, x_r, si_s, si_r, st_s, st_r, qp_s, qp_r, qg_s, qg_r,
    ob_s, ob_r, ls_s, ls_r, op_s, op_r, sm_s, sm_r, ng_s, ng_r,
    lp_s, lp_r, ag_s, ag_r, dp_s, dp_r,
):
    f32, bf16 = jnp.float32, jnp.bfloat16
    me = lax.axis_index("db")
    hs = lax.axis_index("head") * 2 + lax.axis_index("sub")
    rows, width = act.shape
    heads = wq.shape[1] // HDIM
    store = kvs.shape[0]

    def db_at(k):
        return lax.rem(me + k, 4)

    def hs_at(k):
        return lax.rem(hs + k, 4)

    def db_copy(src, dst, send, recv, k):
        return pltpu.make_async_remote_copy(
            src_ref=src, dst_ref=dst, send_sem=send, recv_sem=recv,
            device_id={"db": db_at(k)}, device_id_type=pl.DeviceIdType.MESH,
        )

    def hs_copy(src, dst, send, recv, k):
        peer = hs_at(k)
        return pltpu.make_async_remote_copy(
            src_ref=src, dst_ref=dst, send_sem=send, recv_sem=recv,
            device_id={"head": lax.div(peer, 2), "sub": lax.rem(peer, 2)},
            device_id_type=pl.DeviceIdType.MESH,
        )

    loads = [
        pltpu.make_async_copy(wq_hbm, wq, local_sem.at[0]),
        pltpu.make_async_copy(wo_hbm, wd.at[0], local_sem.at[1]),
        pltpu.make_async_copy(kv_hbm, kvs, local_sem.at[2]),
        pltpu.make_async_copy(wu_hbm, wu, local_sem.at[3]),
    ]
    for c in range(1, 4):
        loads.append(
            pltpu.make_async_copy(wd_hbm.at[pl.ds(c * 1024, 1024)], wd.at[c], local_sem.at[3 + c])
        )
    for load in loads:
        load.start()

    barrier = pltpu.get_barrier_semaphore()
    for k in (1, 2, 3):
        pl.semaphore_signal(
            barrier, inc=1, device_id={"db": db_at(k)}, device_id_type=pl.DeviceIdType.MESH
        )
        peer = hs_at(k)
        pl.semaphore_signal(
            barrier, inc=1, device_id={"head": lax.div(peer, 2), "sub": lax.rem(peer, 2)},
            device_id_type=pl.DeviceIdType.MESH,
        )
    pl.semaphore_wait(barrier, 6)

    sends = []

    def go(copy):
        copy.start()
        sends.append(copy)
        return copy

    def row_sums(values):
        total = jnp.sum(values, axis=1, keepdims=True)
        square = jnp.sum(values * values, axis=1, keepdims=True)
        return jnp.concatenate(
            [jnp.broadcast_to(total, (rows, 128)), jnp.broadcast_to(square, (rows, 128))], axis=1
        )

    def mean_and_scale(sums):
        row_mean = sums[:, 0:1] / D
        row_var = sums[:, 128:129] / D - row_mean * row_mean
        return row_mean, lax.rsqrt(row_var + 1e-05)

    xs = [go(hs_copy(act, xg.at[hs], x_s.at[k - 1], x_r.at[k - 1], k)) for k in (1, 2, 3)]
    st_in[me] = row_sums(act[...].astype(f32))
    copies = [go(db_copy(st_in.at[me], st_in.at[me], si_s.at[k - 1], si_r.at[k - 1], k)) for k in (1, 2, 3)]
    xg[hs] = act[...]
    for copy in copies:
        copy.wait_recv()
    st_tot[hs] = st_in[0] + st_in[1] + st_in[2] + st_in[3]
    copies = [go(hs_copy(st_tot.at[hs], st_tot.at[hs], st_s.at[k - 1], st_r.at[k - 1], k)) for k in (1, 2, 3)]
    for copy in copies:
        copy.wait_recv()
    for copy in xs:
        copy.wait_recv()

    all_mean, all_scale = mean_and_scale(st_tot[...].reshape(4 * rows, 256))

    def norm_tile(t, carry):
        cols = pl.ds(pl.multiple_of(t * 512, 512), 512)
        values = xg[:, :, cols].reshape(4 * rows, 512).astype(f32)
        values = (values - all_mean) * all_scale
        nx[:, cols] = pltpu.roll(values, 4 * rows - (rows - 1), 0).astype(bf16)
        return carry

    lax.fori_loop(0, width // 512, norm_tile, 0)

    loads[0].wait()

    def query_tile(t, carry):
        cols = pl.ds(pl.multiple_of(t * 512, 512), 512)
        qp[:, :, cols] = dot(nx[...], wq[:, cols]).astype(bf16).reshape(4, rows, 512)
        return carry

    lax.fori_loop(0, wq.shape[1] // 512, query_tile, 0)
    copies = [
        go(db_copy(qp.at[db_at(k)], qr.at[me], qp_s.at[k - 1], qp_r.at[k - 1], k)) for k in (1, 2, 3)
    ]
    for copy in copies:
        copy.wait_recv()
    total = qp[me].astype(f32)
    for k in (1, 2, 3):
        total = total + qr[db_at(k)].astype(f32)
    qg[me] = total.astype(bf16)
    copies = [go(db_copy(qg.at[me], qg.at[me], qg_s.at[k - 1], qg_r.at[k - 1], k)) for k in (1, 2, 3)]
    loads[2].wait()
    for copy in copies:
        copy.wait_recv()

    def spot(a, n):
        return place[near[a, n]]

    def owner(a, n):
        return lax.div(spot(a, n), store)

    odd = jnp.where((owner(1, 0) == me) | (owner(1, 1) == me), 1, 0)
    lane = lax.broadcasted_iota(jnp.int32, (rows, 128), 1)
    logs = jnp.zeros((rows, 128), f32)
    for r in range(2):
        span = 2 * r + odd
        which = jnp.where(owner(span, 1) == me, 1, 0)
        slot = lax.rem(spot(span, which), store)
        for h in range(heads):
            cols = slice(h * HDIM, (h + 1) * HDIM)
            scores = lax.dot_general(
                qg[span, :, cols], kvs[slot, 0, :, cols], (((1,), (1,)), ((), ())),
                preferred_element_type=f32,
            ) * HDIM ** (-0.5)
            top = jnp.max(scores, axis=1, keepdims=True)
            raised = jnp.exp(scores - top)
            norm = jnp.sum(raised, axis=1, keepdims=True)
            ob[me, r, :, cols] = dot(
                (raised / norm).astype(bf16), kvs[slot, 1, :, cols]
            ).astype(bf16)
            logs = jnp.where(lane == r * heads + h, top + jnp.log(norm), logs)
    lse[me] = logs
    copies = []
    for k in (1, 2, 3):
        copies.append(go(db_copy(lse.at[me], lse.at[me], ls_s.at[k - 1], ls_r.at[k - 1], k)))
        copies.append(go(db_copy(ob.at[me], ob.at[me], ob_s.at[k - 1], ob_r.at[k - 1], k)))
    loads[1].wait()
    for copy in copies:
        copy.wait_recv()
    for a in range(4):
        r = a // 2
        first, second = owner(a, 0), owner(a, 1)
        log_a, log_b = lse[first], lse[second]
        for h in range(heads):
            cols = slice(h * HDIM, (h + 1) * HDIM)
            at = r * heads + h
            gap = log_b[:, at:at + 1] - log_a[:, at:at + 1]
            mixed = ob[first, r, :, cols].astype(f32) / (1.0 + jnp.exp(gap)) + ob[
                second, r, :, cols
            ].astype(f32) / (1.0 + jnp.exp(-gap))
            att[a * rows:(a + 1) * rows, cols] = mixed.astype(bf16)

    def out_tile(t, carry):
        cols = pl.ds(pl.multiple_of(t * 512, 512), 512)
        part = pltpu.roll(dot(att[...], wd[0, :, cols]), rows - 1, 0)
        row_id = lax.broadcasted_iota(jnp.int32, part.shape, 0)
        part = jnp.where(row_id < rows - 1, 0.0, part)
        op[:, :, cols] = part.astype(bf16).reshape(4, rows, 512)
        return carry

    lax.fori_loop(0, width // 512, out_tile, 0)
    copies = [
        go(hs_copy(op.at[hs_at(k)], orx.at[hs], op_s.at[k - 1], op_r.at[k - 1], k)) for k in (1, 2, 3)
    ]
    first_down = pltpu.make_async_copy(wd_hbm.at[pl.ds(0, 1024)], wd.at[0], wd0_sem)
    first_down.start()
    for copy in copies:
        copy.wait_recv()
    total = act[...].astype(f32) + op[hs].astype(f32)
    for k in (1, 2, 3):
        total = total + orx[hs_at(k)].astype(f32)
    state[...] = total
    st_mid[me] = row_sums(total)
    copies = [go(db_copy(st_mid.at[me], st_mid.at[me], sm_s.at[k - 1], sm_r.at[k - 1], k)) for k in (1, 2, 3)]
    for copy in copies:
        copy.wait_recv()
    row_mean, row_scale = mean_and_scale(st_mid[0] + st_mid[1] + st_mid[2] + st_mid[3])
    ng[hs] = ((state[...] - row_mean) * row_scale).astype(bf16)
    copies = [go(hs_copy(ng.at[hs], ng.at[hs], ng_s.at[k - 1], ng_r.at[k - 1], k)) for k in (1, 2, 3)]
    loads[3].wait()
    for copy in copies:
        copy.wait_recv()

    def lift_copy(c, k):
        return db_copy(
            lp.at[c, db_at(k)], lr.at[c, me], lp_s.at[c, k - 1], lp_r.at[c, k - 1], k
        )

    def up_tile(c, carry):
        for half in range(2):
            cols = pl.ds(pl.multiple_of(c * 1024 + half * 512, 512), 512)
            part = dot(ng[...].reshape(4 * rows, width), wu[:, cols])
            lp[c, :, :, half * 512:(half + 1) * 512] = part.astype(bf16).reshape(4, rows, 512)
        for k in (1, 2, 3):
            lift_copy(c, k).start()
        return carry

    lax.fori_loop(0, 4, up_tile, 0)

    def lifted_copy(c, k):
        return db_copy(ag.at[c, me], ag.at[c, me], ag_s.at[c, k - 1], ag_r.at[c, k - 1], k)

    def gelu_tile(c, carry):
        for k in (1, 2, 3):
            lift_copy(c, k).wait()
        for half in range(2):
            cols = slice(half * 512, (half + 1) * 512)
            total = lp[c, me, :, cols].astype(f32)
            for k in (1, 2, 3):
                total = total + lr[c, db_at(k), :, cols].astype(f32)
            ag[c, me, :, cols] = jax.nn.gelu(total, approximate=True).astype(bf16)
        for k in (1, 2, 3):
            lifted_copy(c, k).start()
        return carry

    lax.fori_loop(0, 4, gelu_tile, 0)

    acc[...] = jnp.zeros_like(acc)
    first_down.wait()
    for load in loads[4:]:
        load.wait()

    def down_tile(c, carry):
        for k in (1, 2, 3):
            lifted_copy(c, k).wait()
        for t in range(4):
            cols = slice(t * 512, (t + 1) * 512)
            acc[:, cols] += dot(ag[c].reshape(4 * rows, 1024), wd[c, :, cols])
        return carry

    lax.fori_loop(0, 4, down_tile, 0)
    dp[...] = acc[...].astype(bf16).reshape(dp.shape)
    copies = [
        go(hs_copy(dp.at[hs_at(k)], dr.at[hs], dp_s.at[k - 1], dp_r.at[k - 1], k)) for k in (1, 2, 3)
    ]
    for copy in copies:
        copy.wait_recv()
    total = state[...] + dp[hs].astype(f32)
    for k in (1, 2, 3):
        total = total + dr[hs_at(k)].astype(f32)
    out[...] = total.astype(bf16)
    for copy in sends:
        copy.wait_send()


def fused(activations, w_query, w_out, w_up, w_down, kv_store, neighbours, block_place):
    f32, bf16 = jnp.float32, jnp.bfloat16
    rows, width = activations.shape
    qw = w_query.shape[1]
    hidden = w_up.shape[1]
    vmem = pl.BlockSpec(memory_space=pltpu.VMEM)
    smem = pl.BlockSpec(memory_space=pltpu.SMEM)
    hbm = pl.BlockSpec(memory_space=pl.ANY)
    tile = hidden // 4
    scratch = [
        pltpu.VMEM(w_query.shape, bf16),
        pltpu.VMEM(w_up.shape, bf16),
        pltpu.VMEM((4, tile, width), bf16),
        pltpu.VMEM(kv_store.shape, bf16),
        pltpu.VMEM((4, rows, width), bf16),
        pltpu.VMEM((4, rows, 256), f32),
        pltpu.VMEM((4, rows, 256), f32),
        pltpu.VMEM((4 * rows, width), bf16),
        pltpu.VMEM((4, rows, qw), bf16),
        pltpu.VMEM((4, rows, qw), bf16),
        pltpu.VMEM((4, rows, qw), bf16),
        pltpu.VMEM((4, 2, rows, qw), bf16),
        pltpu.VMEM((4, rows, 128), f32),
        pltpu.VMEM((4 * rows, qw), bf16),
        pltpu.VMEM((4, rows, width), bf16),
        pltpu.VMEM((4, rows, width), bf16),
        pltpu.VMEM((rows, width), f32),
        pltpu.VMEM((4, rows, 256), f32),
        pltpu.VMEM((4, rows, width), bf16),
        pltpu.VMEM((4, 4, rows, tile), bf16),
        pltpu.VMEM((4, 4, rows, tile), bf16),
        pltpu.VMEM((4, 4, rows, tile), bf16),
        pltpu.VMEM((4 * rows, width), f32),
        pltpu.VMEM((4, rows, width), bf16),
        pltpu.VMEM((4, rows, width), bf16),
        pltpu.SemaphoreType.DMA((7,)),
        pltpu.SemaphoreType.DMA,
    ]
    scratch += [pltpu.SemaphoreType.DMA((3,)) for _ in range(20)]
    scratch += [pltpu.SemaphoreType.DMA((4, 3)) for _ in range(4)]
    scratch += [pltpu.SemaphoreType.DMA((3,)) for _ in range(2)]
    return pl.pallas_call(
        layer_kernel,
        out_shape=jax.ShapeDtypeStruct((rows, width), bf16),
        in_specs=[vmem, hbm, hbm, hbm, hbm, hbm, smem, smem],
        out_specs=vmem,
        scratch_shapes=scratch,
        compiler_params=pltpu.CompilerParams(
            collective_id=0, has_side_effects=True, vmem_limit_bytes=VMEM_BYTES
        ),
    )(activations, w_query, w_out, w_up, w_down, kv_store, neighbours, block_place)


def solution(mesh):
    in_specs = (
        P(("grp", "head", "sub"), "db"),
        P("db", ("head", "sub")),
        P(("head", "sub"), "db"),
        P("db", ("head", "sub")),
        P(("head", "sub"), "db"),
        P(("grp", "db"), None, None, ("head", "sub")),
        P("grp", None),
        P("grp"),
    )
    out_specs = P(("grp", "head", "sub"), "db")
    sizes = mesh.shape
    body = fused if (sizes["db"], sizes["head"], sizes["sub"]) == (4, 2, 2) else local
    return jax.shard_map(body, mesh=mesh, in_specs=in_specs, out_specs=out_specs, check_vma=False)
```

```python
import jax
import jax.numpy as jnp
from jax import lax
from jax.experimental import pallas as pl
from jax.experimental.pallas import tpu as pltpu
from jax.sharding import PartitionSpec as P

D = 8192
HDIM = 128
NEIGH = 2
NTOK = 128
PIECES = 16
VMEM_BYTES = 63 * 1024 * 1024


def apply_norm(values, row_sums):
    row_mean = row_sums[0] / D
    row_var = row_sums[1] / D - row_mean * row_mean
    return ((values - row_mean) * lax.rsqrt(row_var + 1e-05)).astype(jnp.bfloat16)


def local(activations, w_query, w_out, w_up, w_down, kv_store, neighbours, block_place):
    shards = lax.axis_size("db")
    my_index = lax.axis_index("db")
    inputs = lax.all_gather(activations, ("head", "sub"), axis=0, tiled=True).astype(jnp.float32)
    sums_in = lax.psum(
        (jnp.sum(inputs, axis=1, keepdims=True), jnp.sum(inputs * inputs, axis=1, keepdims=True)),
        "db",
    )
    normed = apply_norm(inputs, sums_in)
    queries = lax.psum_scatter(
        jnp.dot(normed, w_query, preferred_element_type=jnp.float32),
        "db",
        scatter_dimension=0,
        tiled=True,
    ).astype(jnp.bfloat16)
    local_width = queries.shape[1]
    head_count = local_width // HDIM
    span_rows = queries.shape[0]
    earlier = lax.dynamic_slice_in_dim(neighbours, jnp.maximum(my_index - 1, 0), 1, 0)
    current = lax.dynamic_slice_in_dim(neighbours, my_index, 1, 0)
    wanted = jnp.concatenate([earlier, current], 0).reshape(-1)
    block_ids = jnp.arange(block_place.shape[0], dtype=jnp.int32)
    located = jnp.sum(
        jnp.where(block_ids[None, :] == wanted[:, None], block_place[None, :], 0), axis=1
    )
    store_blocks = kv_store.shape[0]
    owner_of = located // store_blocks
    slot_of = located % store_blocks
    request_ids = jnp.arange(2 * NEIGH, dtype=jnp.int32)
    segment_of = (request_ids >= NEIGH).astype(jnp.int32)
    usable = jnp.where(request_ids < NEIGH, my_index > 0, True)
    peer_ids = jnp.arange(shards, dtype=jnp.int32)
    coded_slot = 2 * slot_of + segment_of + 1
    request_out = (
        jnp.sum(
            jnp.where(
                (owner_of[None, :] == peer_ids[:, None]) & usable[None, :], coded_slot[None, :], 0
            ),
            axis=1,
            keepdims=True,
        )
        - 1
    )
    request_in = lax.all_to_all(request_out, "db", split_axis=0, concat_axis=0, tiled=True)
    asked_for = request_in[:, 0]
    chosen_slot = jnp.maximum(asked_for, 0) // 2
    row_index = jnp.arange(span_rows, dtype=jnp.int32)
    row_segment = (row_index == span_rows - 1).astype(jnp.int32)
    row_live = (row_index == span_rows - 1) | (my_index > 0)
    score_scale = HDIM ** (-0.5)
    outgoing = jnp.take(kv_store, chosen_slot, axis=0)
    outgoing = jnp.where((asked_for >= 0)[:, None, None, None], outgoing, jnp.zeros_like(outgoing))
    arrived = lax.all_to_all(outgoing, "db", split_axis=0, concat_axis=0, tiled=True)
    needed = jnp.take(arrived, owner_of, axis=0)
    key_block = needed[:, 0].reshape(-1, head_count, HDIM)
    value_block = needed[:, 1].reshape(-1, head_count, HDIM)
    query_heads = queries.reshape(span_rows, head_count, HDIM)
    scores = (
        jnp.einsum("rhe,khe->hrk", query_heads, key_block, preferred_element_type=jnp.float32)
        * score_scale
    )
    key_request = jnp.arange(key_block.shape[0], dtype=jnp.int32) // NTOK
    key_live = (segment_of[key_request][None, :] == row_segment[:, None]) & usable[key_request][
        None, :
    ]
    scores = jnp.where(key_live[None], scores, -1e30)
    top_score = jnp.max(scores, axis=-1, keepdims=True)
    exponent = jnp.exp(scores - top_score)
    weights = (exponent / jnp.sum(exponent, axis=-1, keepdims=True)).astype(jnp.bfloat16)
    attended = jnp.einsum("hrk,khe->rhe", weights, value_block, preferred_element_type=jnp.float32)
    attended = attended.reshape(span_rows, local_width).astype(jnp.bfloat16)
    attended = jnp.where(row_live[:, None], attended, jnp.zeros_like(attended))
    attn_part = jnp.dot(
        lax.all_gather(attended, "db", axis=0, tiled=True),
        w_out,
        preferred_element_type=jnp.float32,
    )
    attn_full = lax.psum(attn_part, ("head", "sub"))
    state_rows = inputs + attn_full
    sums_mid = lax.psum(
        (
            jnp.sum(state_rows, axis=1, keepdims=True),
            jnp.sum(state_rows * state_rows, axis=1, keepdims=True),
        ),
        "db",
    )
    normed_mid = apply_norm(state_rows, sums_mid)
    lifted = lax.psum_scatter(
        jnp.dot(normed_mid, w_up, preferred_element_type=jnp.float32).astype(jnp.bfloat16),
        "db",
        scatter_dimension=0,
        tiled=True,
    ).astype(jnp.float32)
    activated = jax.nn.gelu(lifted, approximate=True).astype(jnp.bfloat16)
    gathered = lax.all_gather(activated, "db", axis=0, tiled=True)
    group_rows = state_rows.shape[0] // lax.axis_size(("head", "sub"))
    lowered = lax.psum_scatter(
        jnp.dot(gathered, w_down, preferred_element_type=jnp.float32).astype(jnp.bfloat16),
        ("head", "sub"),
        scatter_dimension=0,
        tiled=True,
    ).astype(jnp.float32)
    own_state = lax.dynamic_slice_in_dim(
        state_rows, lax.axis_index(("head", "sub")) * group_rows, group_rows, 0
    )
    return (own_state + lowered).astype(jnp.bfloat16)


def dot(left, right):
    return jnp.dot(left, right, preferred_element_type=jnp.float32)


def layer_kernel(
    act, wq_hbm, wo_hbm, wu_hbm, wd_hbm, kv_hbm, near, place, out,
    wq, wu, wd, kvs, xg, st_in, st_tot, nx, qp, qr, qg, ob, lse, att,
    op, orx, state, st_mid, ng, lp, lr, ag, acc, dp, dr,
    local_sem, wd0_sem, x_s, x_r, si_s, si_r, st_s, st_r, qp_s, qp_r, qg_s, qg_r,
    ob_s, ob_r, ls_s, ls_r, op_s, op_r, sm_s, sm_r, ng_s, ng_r, dp_s, dp_r,
    lp_s, lp_r, ag_s, ag_r,
):
    f32, bf16 = jnp.float32, jnp.bfloat16
    me = lax.axis_index("db")
    hs = lax.axis_index("head") * 2 + lax.axis_index("sub")
    rows, width = act.shape
    heads = wq.shape[1] // HDIM
    store = kvs.shape[0]

    def db_at(k):
        return lax.rem(me + k, 4)

    def hs_at(k):
        return lax.rem(hs + k, 4)

    def db_copy(src, dst, send, recv, k):
        return pltpu.make_async_remote_copy(
            src_ref=src, dst_ref=dst, send_sem=send, recv_sem=recv,
            device_id={"db": db_at(k)}, device_id_type=pl.DeviceIdType.MESH,
        )

    def hs_copy(src, dst, send, recv, k):
        peer = hs_at(k)
        return pltpu.make_async_remote_copy(
            src_ref=src, dst_ref=dst, send_sem=send, recv_sem=recv,
            device_id={"head": lax.div(peer, 2), "sub": lax.rem(peer, 2)},
            device_id_type=pl.DeviceIdType.MESH,
        )

    loads = [
        pltpu.make_async_copy(wq_hbm, wq, local_sem.at[0]),
        pltpu.make_async_copy(wo_hbm, wd.at[pl.ds(0, 1024)], local_sem.at[1]),
        pltpu.make_async_copy(kv_hbm, kvs, local_sem.at[2]),
        pltpu.make_async_copy(wu_hbm, wu, local_sem.at[3]),
    ]
    for c in range(1, 4):
        loads.append(
            pltpu.make_async_copy(wd_hbm.at[pl.ds(c * 1024, 1024)], wd.at[pl.ds(c * 1024, 1024)], local_sem.at[3 + c])
        )
    for load in loads:
        load.start()

    barrier = pltpu.get_barrier_semaphore()
    for k in (1, 2, 3):
        pl.semaphore_signal(
            barrier, inc=1, device_id={"db": db_at(k)}, device_id_type=pl.DeviceIdType.MESH
        )
        peer = hs_at(k)
        pl.semaphore_signal(
            barrier, inc=1, device_id={"head": lax.div(peer, 2), "sub": lax.rem(peer, 2)},
            device_id_type=pl.DeviceIdType.MESH,
        )
    pl.semaphore_wait(barrier, 6)

    sends = []

    def go(copy):
        copy.start()
        sends.append(copy)
        return copy

    head, sub = lax.axis_index("head"), lax.axis_index("sub")
    across = (1 - head) * 2 + sub
    beside = head * 2 + 1 - sub
    far = (1 - head) * 2 + 1 - sub

    def send_across(src, dst, send, recv):
        return pltpu.make_async_remote_copy(
            src_ref=src, dst_ref=dst, send_sem=send, recv_sem=recv,
            device_id={"head": 1 - head}, device_id_type=pl.DeviceIdType.MESH,
        )

    def send_beside(src, dst, send, recv):
        return pltpu.make_async_remote_copy(
            src_ref=src, dst_ref=dst, send_sem=send, recv_sem=recv,
            device_id={"sub": 1 - sub}, device_id_type=pl.DeviceIdType.MESH,
        )

    def spread(own, buffer, send, recv):
        first = go(send_across(own, buffer.at[hs], send.at[0], recv.at[0]))
        second = go(send_beside(own, buffer.at[hs], send.at[1], recv.at[1]))

        def finish():
            first.wait_recv()
            third = go(
                send_beside(buffer.at[across], buffer.at[across], send.at[2], recv.at[2])
            )
            second.wait_recv()
            third.wait_recv()

        return finish

    def reduce_to_owner(parts, landing, send, recv):
        first = go(send_beside(parts.at[far], landing.at[0], send.at[0], recv.at[0]))
        second = go(send_beside(parts.at[beside], landing.at[1], send.at[1], recv.at[1]))
        first.wait_recv()
        parts[across] = (parts[across].astype(f32) + landing[0].astype(f32)).astype(bf16)
        third = go(send_across(parts.at[across], landing.at[2], send.at[2], recv.at[2]))
        second.wait_recv()
        total = parts[hs].astype(f32) + landing[1].astype(f32)
        third.wait_recv()
        return total + landing[2].astype(f32)

    def row_sums(values):
        total = jnp.sum(values, axis=1, keepdims=True)
        square = jnp.sum(values * values, axis=1, keepdims=True)
        return jnp.concatenate(
            [jnp.broadcast_to(total, (rows, 128)), jnp.broadcast_to(square, (rows, 128))], axis=1
        )

    def mean_and_scale(sums):
        row_mean = sums[:, 0:1] / D
        row_var = sums[:, 128:129] / D - row_mean * row_mean
        return row_mean, lax.rsqrt(row_var + 1e-05)

    finish = spread(act, xg, x_s, x_r)
    st_in[me] = row_sums(act[...].astype(f32))
    copies = [go(db_copy(st_in.at[me], st_in.at[me], si_s.at[k - 1], si_r.at[k - 1], k)) for k in (1, 2, 3)]
    xg[hs] = act[...]
    for copy in copies:
        copy.wait_recv()
    st_tot[hs] = st_in[0] + st_in[1] + st_in[2] + st_in[3]
    copies = [go(hs_copy(st_tot.at[hs], st_tot.at[hs], st_s.at[k - 1], st_r.at[k - 1], k)) for k in (1, 2, 3)]
    for copy in copies:
        copy.wait_recv()
    finish()

    all_mean, all_scale = mean_and_scale(st_tot[...].reshape(4 * rows, 256))

    def norm_tile(t, carry):
        cols = pl.ds(pl.multiple_of(t * 512, 512), 512)
        values = xg[:, :, cols].reshape(4 * rows, 512).astype(f32)
        values = (values - all_mean) * all_scale
        nx[:, cols] = pltpu.roll(values, 4 * rows - (rows - 1), 0).astype(bf16)
        return carry

    lax.fori_loop(0, width // 512, norm_tile, 0)

    loads[0].wait()

    def query_tile(t, carry):
        cols = pl.ds(pl.multiple_of(t * 512, 512), 512)
        qp[:, :, cols] = dot(nx[...], wq[:, cols]).astype(bf16).reshape(4, rows, 512)
        return carry

    lax.fori_loop(0, wq.shape[1] // 512, query_tile, 0)
    copies = [
        go(db_copy(qp.at[db_at(k)], qr.at[me], qp_s.at[k - 1], qp_r.at[k - 1], k)) for k in (1, 2, 3)
    ]
    for copy in copies:
        copy.wait_recv()
    total = qp[me].astype(f32)
    for k in (1, 2, 3):
        total = total + qr[db_at(k)].astype(f32)
    qg[me] = total.astype(bf16)
    copies = [go(db_copy(qg.at[me], qg.at[me], qg_s.at[k - 1], qg_r.at[k - 1], k)) for k in (1, 2, 3)]
    loads[2].wait()
    for copy in copies:
        copy.wait_recv()

    def spot(a, n):
        return place[near[a, n]]

    def owner(a, n):
        return lax.div(spot(a, n), store)

    odd = jnp.where((owner(1, 0) == me) | (owner(1, 1) == me), 1, 0)
    lane = lax.broadcasted_iota(jnp.int32, (rows, 128), 1)
    logs = jnp.zeros((rows, 128), f32)
    for r in range(2):
        span = 2 * r + odd
        which = jnp.where(owner(span, 1) == me, 1, 0)
        slot = lax.rem(spot(span, which), store)
        for h in range(heads):
            cols = slice(h * HDIM, (h + 1) * HDIM)
            scores = lax.dot_general(
                qg[span, :, cols], kvs[slot, 0, :, cols], (((1,), (1,)), ((), ())),
                preferred_element_type=f32,
            ) * HDIM ** (-0.5)
            top = jnp.max(scores, axis=1, keepdims=True)
            raised = jnp.exp(scores - top)
            norm = jnp.sum(raised, axis=1, keepdims=True)
            ob[me, r, :, cols] = dot(
                (raised / norm).astype(bf16), kvs[slot, 1, :, cols]
            ).astype(bf16)
            logs = jnp.where(lane == r * heads + h, top + jnp.log(norm), logs)
    lse[me] = logs
    copies = []
    for k in (1, 2, 3):
        copies.append(go(db_copy(lse.at[me], lse.at[me], ls_s.at[k - 1], ls_r.at[k - 1], k)))
        copies.append(go(db_copy(ob.at[me], ob.at[me], ob_s.at[k - 1], ob_r.at[k - 1], k)))
    loads[1].wait()
    for copy in copies:
        copy.wait_recv()
    for a in range(4):
        r = a // 2
        first, second = owner(a, 0), owner(a, 1)
        log_a, log_b = lse[first], lse[second]
        for h in range(heads):
            cols = slice(h * HDIM, (h + 1) * HDIM)
            at = r * heads + h
            gap = log_b[:, at:at + 1] - log_a[:, at:at + 1]
            mixed = ob[first, r, :, cols].astype(f32) / (1.0 + jnp.exp(gap)) + ob[
                second, r, :, cols
            ].astype(f32) / (1.0 + jnp.exp(-gap))
            att[a * rows:(a + 1) * rows, cols] = mixed.astype(bf16)

    def out_tile(t, carry):
        cols = pl.ds(pl.multiple_of(t * 512, 512), 512)
        part = pltpu.roll(dot(att[...], wd[pl.ds(0, 1024), cols]), rows - 1, 0)
        row_id = lax.broadcasted_iota(jnp.int32, part.shape, 0)
        part = jnp.where(row_id < rows - 1, 0.0, part)
        op[:, :, cols] = part.astype(bf16).reshape(4, rows, 512)
        return carry

    lax.fori_loop(0, width // 512, out_tile, 0)
    total = act[...].astype(f32) + reduce_to_owner(op, orx, op_s, op_r)
    first_down = pltpu.make_async_copy(
        wd_hbm.at[pl.ds(0, 1024)], wd.at[pl.ds(0, 1024)], wd0_sem
    )
    first_down.start()
    state[...] = total
    st_mid[me] = row_sums(total)
    copies = [go(db_copy(st_mid.at[me], st_mid.at[me], sm_s.at[k - 1], sm_r.at[k - 1], k)) for k in (1, 2, 3)]
    for copy in copies:
        copy.wait_recv()
    row_mean, row_scale = mean_and_scale(st_mid[0] + st_mid[1] + st_mid[2] + st_mid[3])
    ng[hs] = ((state[...] - row_mean) * row_scale).astype(bf16)
    finish = spread(ng.at[hs], ng, ng_s, ng_r)
    loads[3].wait()

    finish()

    pieces, wide = lp.shape[1], lp.shape[3]
    half = 2 * rows
    first_down.wait()
    for load in loads[4:]:
        load.wait()
    acc[...] = jnp.zeros_like(acc)
    lines = ((me, lax.rem(me + 1, 4), lax.rem(me + 3, 4)), (3 - me, lax.rem(me + 3, 4), lax.rem(me + 1, 4)))

    def along(src, dst, send, recv, peer):
        return pltpu.make_async_remote_copy(
            src_ref=src, dst_ref=dst, send_sem=send, recv_sem=recv,
            device_id={"db": peer}, device_id_type=pl.DeviceIdType.MESH,
        )

    def sum_copy(way, c, src):
        return along(
            src.at[way, c], lr.at[way, c], lp_s.at[way, c], lp_r.at[way, c], lines[way][1]
        )

    def back_copy(way, c):
        return along(
            ag.at[way, c], ag.at[way, c], ag_s.at[way, c], ag_r.at[way, c], lines[way][2]
        )

    def step(t, carry):
        @pl.when(t < pieces)
        def _():
            cols = pl.ds(pl.multiple_of(t * wide, wide), wide)
            part = dot(ng[...].reshape(4 * rows, width), wu[:, cols])
            lp[:, t] = part.astype(bf16).reshape(2, half, wide)
            for way in range(2):

                @pl.when(lines[way][0] == 0)
                def _():
                    sum_copy(way, t, lp).start()

        for way in range(2):
            spot_on = lines[way][0]
            c = t - (2 * spot_on - 1)

            @pl.when((spot_on > 0) & (c >= 0) & (c < pieces))
            def _():
                sum_copy(way, c, lr).wait_recv()
                total = lr[way, c].astype(f32) + lp[way, c].astype(f32)

                @pl.when(spot_on < 3)
                def _():
                    lr[way, c] = total.astype(bf16)
                    sum_copy(way, c, lr).start()

                @pl.when(spot_on == 3)
                def _():
                    ag[way, c] = jax.nn.gelu(total, approximate=True).astype(bf16)
                    back_copy(way, c).start()

        for way in range(2):
            spot_on = lines[way][0]
            c = t - 11 + 2 * spot_on

            @pl.when((c >= 0) & (c < pieces))
            def _():
                @pl.when(spot_on < 3)
                def _():
                    back_copy(way, c).wait_recv()

                    @pl.when(spot_on > 0)
                    def _():
                        back_copy(way, c).start()

                deep = pl.ds(pl.multiple_of(c * wide, wide), wide)
                for n in range(width // 512):
                    cols = slice(n * 512, (n + 1) * 512)
                    acc[way * half:(way + 1) * half, cols] += dot(ag[way, c], wd[deep, cols])

        return carry

    lax.fori_loop(0, pieces + 11, step, 0)
    dp[...] = acc[...].astype(bf16).reshape(dp.shape)
    total = reduce_to_owner(dp, dr, dp_s, dp_r)
    out[...] = (state[...] + total).astype(bf16)

    def drain(c, carry):
        for way in range(2):

            @pl.when(lines[way][0] < 3)
            def _():
                sum_copy(way, c, lr).wait_send()

            @pl.when(lines[way][0] > 0)
            def _():
                back_copy(way, c).wait_send()

        return carry

    lax.fori_loop(0, pieces, drain, 0)
    for copy in sends:
        copy.wait_send()


def fused(activations, w_query, w_out, w_up, w_down, kv_store, neighbours, block_place):
    f32, bf16 = jnp.float32, jnp.bfloat16
    rows, width = activations.shape
    qw = w_query.shape[1]
    hidden = w_up.shape[1]
    vmem = pl.BlockSpec(memory_space=pltpu.VMEM)
    smem = pl.BlockSpec(memory_space=pltpu.SMEM)
    hbm = pl.BlockSpec(memory_space=pl.ANY)
    wide = hidden // PIECES
    scratch = [
        pltpu.VMEM(w_query.shape, bf16),
        pltpu.VMEM(w_up.shape, bf16),
        pltpu.VMEM((hidden, width), bf16),
        pltpu.VMEM(kv_store.shape, bf16),
        pltpu.VMEM((4, rows, width), bf16),
        pltpu.VMEM((4, rows, 256), f32),
        pltpu.VMEM((4, rows, 256), f32),
        pltpu.VMEM((4 * rows, width), bf16),
        pltpu.VMEM((4, rows, qw), bf16),
        pltpu.VMEM((4, rows, qw), bf16),
        pltpu.VMEM((4, rows, qw), bf16),
        pltpu.VMEM((4, 2, rows, qw), bf16),
        pltpu.VMEM((4, rows, 128), f32),
        pltpu.VMEM((4 * rows, qw), bf16),
        pltpu.VMEM((4, rows, width), bf16),
        pltpu.VMEM((3, rows, width), bf16),
        pltpu.VMEM((rows, width), f32),
        pltpu.VMEM((4, rows, 256), f32),
        pltpu.VMEM((4, rows, width), bf16),
        pltpu.VMEM((2, PIECES, 2 * rows, wide), bf16),
        pltpu.VMEM((2, PIECES, 2 * rows, wide), bf16),
        pltpu.VMEM((2, PIECES, 2 * rows, wide), bf16),
        pltpu.VMEM((4 * rows, width), f32),
        pltpu.VMEM((4, rows, width), bf16),
        pltpu.VMEM((3, rows, width), bf16),
        pltpu.SemaphoreType.DMA((7,)),
        pltpu.SemaphoreType.DMA,
    ]
    scratch += [pltpu.SemaphoreType.DMA((3,)) for _ in range(22)]
    scratch += [pltpu.SemaphoreType.DMA((2, PIECES)) for _ in range(4)]
    return pl.pallas_call(
        layer_kernel,
        out_shape=jax.ShapeDtypeStruct((rows, width), bf16),
        in_specs=[vmem, hbm, hbm, hbm, hbm, hbm, smem, smem],
        out_specs=vmem,
        scratch_shapes=scratch,
        compiler_params=pltpu.CompilerParams(
            collective_id=0, has_side_effects=True, vmem_limit_bytes=VMEM_BYTES
        ),
    )(activations, w_query, w_out, w_up, w_down, kv_store, neighbours, block_place)


def solution(mesh):
    in_specs = (
        P(("grp", "head", "sub"), "db"),
        P("db", ("head", "sub")),
        P(("head", "sub"), "db"),
        P("db", ("head", "sub")),
        P(("head", "sub"), "db"),
        P(("grp", "db"), None, None, ("head", "sub")),
        P("grp", None),
        P("grp"),
    )
    out_specs = P(("grp", "head", "sub"), "db")
    sizes = mesh.shape
    body = fused if (sizes["db"], sizes["head"], sizes["sub"]) == (4, 2, 2) else local
    return jax.shard_map(body, mesh=mesh, in_specs=in_specs, out_specs=out_specs, check_vma=False)
```

```python
import jax
import jax.numpy as jnp
from jax import lax
from jax.experimental import pallas as pl
from jax.experimental.pallas import tpu as pltpu
from jax.sharding import PartitionSpec as P

D = 8192
HDIM = 128
NEIGH = 2
NTOK = 128
PIECES = 16
VMEM_BYTES = 63 * 1024 * 1024


def apply_norm(values, row_sums):
    row_mean = row_sums[0] / D
    row_var = row_sums[1] / D - row_mean * row_mean
    return ((values - row_mean) * lax.rsqrt(row_var + 1e-05)).astype(jnp.bfloat16)


def local(activations, w_query, w_out, w_up, w_down, kv_store, neighbours, block_place):
    shards = lax.axis_size("db")
    my_index = lax.axis_index("db")
    inputs = lax.all_gather(activations, ("head", "sub"), axis=0, tiled=True).astype(jnp.float32)
    sums_in = lax.psum(
        (jnp.sum(inputs, axis=1, keepdims=True), jnp.sum(inputs * inputs, axis=1, keepdims=True)),
        "db",
    )
    normed = apply_norm(inputs, sums_in)
    queries = lax.psum_scatter(
        jnp.dot(normed, w_query, preferred_element_type=jnp.float32),
        "db",
        scatter_dimension=0,
        tiled=True,
    ).astype(jnp.bfloat16)
    local_width = queries.shape[1]
    head_count = local_width // HDIM
    span_rows = queries.shape[0]
    earlier = lax.dynamic_slice_in_dim(neighbours, jnp.maximum(my_index - 1, 0), 1, 0)
    current = lax.dynamic_slice_in_dim(neighbours, my_index, 1, 0)
    wanted = jnp.concatenate([earlier, current], 0).reshape(-1)
    block_ids = jnp.arange(block_place.shape[0], dtype=jnp.int32)
    located = jnp.sum(
        jnp.where(block_ids[None, :] == wanted[:, None], block_place[None, :], 0), axis=1
    )
    store_blocks = kv_store.shape[0]
    owner_of = located // store_blocks
    slot_of = located % store_blocks
    request_ids = jnp.arange(2 * NEIGH, dtype=jnp.int32)
    segment_of = (request_ids >= NEIGH).astype(jnp.int32)
    usable = jnp.where(request_ids < NEIGH, my_index > 0, True)
    peer_ids = jnp.arange(shards, dtype=jnp.int32)
    coded_slot = 2 * slot_of + segment_of + 1
    request_out = (
        jnp.sum(
            jnp.where(
                (owner_of[None, :] == peer_ids[:, None]) & usable[None, :], coded_slot[None, :], 0
            ),
            axis=1,
            keepdims=True,
        )
        - 1
    )
    request_in = lax.all_to_all(request_out, "db", split_axis=0, concat_axis=0, tiled=True)
    asked_for = request_in[:, 0]
    chosen_slot = jnp.maximum(asked_for, 0) // 2
    row_index = jnp.arange(span_rows, dtype=jnp.int32)
    row_segment = (row_index == span_rows - 1).astype(jnp.int32)
    row_live = (row_index == span_rows - 1) | (my_index > 0)
    score_scale = HDIM ** (-0.5)
    outgoing = jnp.take(kv_store, chosen_slot, axis=0)
    outgoing = jnp.where((asked_for >= 0)[:, None, None, None], outgoing, jnp.zeros_like(outgoing))
    arrived = lax.all_to_all(outgoing, "db", split_axis=0, concat_axis=0, tiled=True)
    needed = jnp.take(arrived, owner_of, axis=0)
    key_block = needed[:, 0].reshape(-1, head_count, HDIM)
    value_block = needed[:, 1].reshape(-1, head_count, HDIM)
    query_heads = queries.reshape(span_rows, head_count, HDIM)
    scores = (
        jnp.einsum("rhe,khe->hrk", query_heads, key_block, preferred_element_type=jnp.float32)
        * score_scale
    )
    key_request = jnp.arange(key_block.shape[0], dtype=jnp.int32) // NTOK
    key_live = (segment_of[key_request][None, :] == row_segment[:, None]) & usable[key_request][
        None, :
    ]
    scores = jnp.where(key_live[None], scores, -1e30)
    top_score = jnp.max(scores, axis=-1, keepdims=True)
    exponent = jnp.exp(scores - top_score)
    weights = (exponent / jnp.sum(exponent, axis=-1, keepdims=True)).astype(jnp.bfloat16)
    attended = jnp.einsum("hrk,khe->rhe", weights, value_block, preferred_element_type=jnp.float32)
    attended = attended.reshape(span_rows, local_width).astype(jnp.bfloat16)
    attended = jnp.where(row_live[:, None], attended, jnp.zeros_like(attended))
    attn_part = jnp.dot(
        lax.all_gather(attended, "db", axis=0, tiled=True),
        w_out,
        preferred_element_type=jnp.float32,
    )
    attn_full = lax.psum(attn_part, ("head", "sub"))
    state_rows = inputs + attn_full
    sums_mid = lax.psum(
        (
            jnp.sum(state_rows, axis=1, keepdims=True),
            jnp.sum(state_rows * state_rows, axis=1, keepdims=True),
        ),
        "db",
    )
    normed_mid = apply_norm(state_rows, sums_mid)
    lifted = lax.psum_scatter(
        jnp.dot(normed_mid, w_up, preferred_element_type=jnp.float32).astype(jnp.bfloat16),
        "db",
        scatter_dimension=0,
        tiled=True,
    ).astype(jnp.float32)
    activated = jax.nn.gelu(lifted, approximate=True).astype(jnp.bfloat16)
    gathered = lax.all_gather(activated, "db", axis=0, tiled=True)
    group_rows = state_rows.shape[0] // lax.axis_size(("head", "sub"))
    lowered = lax.psum_scatter(
        jnp.dot(gathered, w_down, preferred_element_type=jnp.float32).astype(jnp.bfloat16),
        ("head", "sub"),
        scatter_dimension=0,
        tiled=True,
    ).astype(jnp.float32)
    own_state = lax.dynamic_slice_in_dim(
        state_rows, lax.axis_index(("head", "sub")) * group_rows, group_rows, 0
    )
    return (own_state + lowered).astype(jnp.bfloat16)


def dot(left, right):
    return jnp.dot(left, right, preferred_element_type=jnp.float32)


def layer_kernel(
    act, wq_hbm, wo_hbm, wu_hbm, wd_hbm, kv_hbm, near, place, out,
    wq, wu, wd, kvs, xg, st_in, st_tot, nx, qp, qr, qg, ob, lse, att,
    op, orx, state, st_mid, ng, lp, lr, ag, acc, dp, dr,
    local_sem, wd0_sem, x_s, x_r, si_s, si_r, st_s, st_r, qp_s, qp_r, qg_s, qg_r,
    ob_s, ob_r, ls_s, ls_r, op_s, op_r, sm_s, sm_r, ng_s, ng_r, dp_s, dp_r,
    lp_s, lp_r, ag_s, ag_r,
):
    f32, bf16 = jnp.float32, jnp.bfloat16
    me = lax.axis_index("db")
    hs = lax.axis_index("head") * 2 + lax.axis_index("sub")
    rows, width = act.shape
    heads = wq.shape[1] // HDIM
    store = kvs.shape[0]

    def db_at(k):
        return lax.rem(me + k, 4)

    def hs_at(k):
        return lax.rem(hs + k, 4)

    def db_copy(src, dst, send, recv, k):
        return pltpu.make_async_remote_copy(
            src_ref=src, dst_ref=dst, send_sem=send, recv_sem=recv,
            device_id={"db": db_at(k)}, device_id_type=pl.DeviceIdType.MESH,
        )

    def hs_copy(src, dst, send, recv, k):
        peer = hs_at(k)
        return pltpu.make_async_remote_copy(
            src_ref=src, dst_ref=dst, send_sem=send, recv_sem=recv,
            device_id={"head": lax.div(peer, 2), "sub": lax.rem(peer, 2)},
            device_id_type=pl.DeviceIdType.MESH,
        )

    loads = [
        pltpu.make_async_copy(wq_hbm, wq, local_sem.at[0]),
        pltpu.make_async_copy(wo_hbm, wd.at[pl.ds(0, 1024)], local_sem.at[1]),
        pltpu.make_async_copy(kv_hbm, kvs, local_sem.at[2]),
        pltpu.make_async_copy(wu_hbm, wu, local_sem.at[3]),
    ]
    for c in range(1, 4):
        loads.append(
            pltpu.make_async_copy(wd_hbm.at[pl.ds(c * 1024, 1024)], wd.at[pl.ds(c * 1024, 1024)], local_sem.at[3 + c])
        )
    for load in loads:
        load.start()

    barrier = pltpu.get_barrier_semaphore()
    for k in (1, 2, 3):
        pl.semaphore_signal(
            barrier, inc=1, device_id={"db": db_at(k)}, device_id_type=pl.DeviceIdType.MESH
        )
        peer = hs_at(k)
        pl.semaphore_signal(
            barrier, inc=1, device_id={"head": lax.div(peer, 2), "sub": lax.rem(peer, 2)},
            device_id_type=pl.DeviceIdType.MESH,
        )
    pl.semaphore_wait(barrier, 6)

    sends = []

    def go(copy):
        copy.start()
        sends.append(copy)
        return copy

    head, sub = lax.axis_index("head"), lax.axis_index("sub")
    across = (1 - head) * 2 + sub
    beside = head * 2 + 1 - sub
    far = (1 - head) * 2 + 1 - sub

    def send_across(src, dst, send, recv):
        return pltpu.make_async_remote_copy(
            src_ref=src, dst_ref=dst, send_sem=send, recv_sem=recv,
            device_id={"head": 1 - head}, device_id_type=pl.DeviceIdType.MESH,
        )

    def send_beside(src, dst, send, recv):
        return pltpu.make_async_remote_copy(
            src_ref=src, dst_ref=dst, send_sem=send, recv_sem=recv,
            device_id={"sub": 1 - sub}, device_id_type=pl.DeviceIdType.MESH,
        )

    def spread(own, buffer, send, recv):
        first = go(send_across(own, buffer.at[hs], send.at[0], recv.at[0]))
        second = go(send_beside(own, buffer.at[hs], send.at[1], recv.at[1]))

        def finish():
            first.wait_recv()
            third = go(
                send_beside(buffer.at[across], buffer.at[across], send.at[2], recv.at[2])
            )
            second.wait_recv()
            third.wait_recv()

        return finish

    def reduce_to_owner(parts, landing, send, recv):
        first = go(send_beside(parts.at[far], landing.at[0], send.at[0], recv.at[0]))
        second = go(send_beside(parts.at[beside], landing.at[1], send.at[1], recv.at[1]))
        first.wait_recv()
        parts[across] = (parts[across].astype(f32) + landing[0].astype(f32)).astype(bf16)
        third = go(send_across(parts.at[across], landing.at[2], send.at[2], recv.at[2]))
        second.wait_recv()
        total = parts[hs].astype(f32) + landing[1].astype(f32)
        third.wait_recv()
        return total + landing[2].astype(f32)

    def row_sums(values):
        total = jnp.sum(values, axis=1, keepdims=True)
        square = jnp.sum(values * values, axis=1, keepdims=True)
        return jnp.concatenate(
            [jnp.broadcast_to(total, (rows, 128)), jnp.broadcast_to(square, (rows, 128))], axis=1
        )

    def mean_and_scale(sums):
        row_mean = sums[:, 0:1] / D
        row_var = sums[:, 128:129] / D - row_mean * row_mean
        return row_mean, lax.rsqrt(row_var + 1e-05)

    finish = spread(act, xg, x_s, x_r)
    st_in[me] = row_sums(act[...].astype(f32))
    copies = [go(db_copy(st_in.at[me], st_in.at[me], si_s.at[k - 1], si_r.at[k - 1], k)) for k in (1, 2, 3)]
    xg[hs] = act[...]
    for copy in copies:
        copy.wait_recv()
    st_tot[hs] = st_in[0] + st_in[1] + st_in[2] + st_in[3]
    copies = [go(hs_copy(st_tot.at[hs], st_tot.at[hs], st_s.at[k - 1], st_r.at[k - 1], k)) for k in (1, 2, 3)]
    for copy in copies:
        copy.wait_recv()
    finish()

    all_mean, all_scale = mean_and_scale(st_tot[...].reshape(4 * rows, 256))

    def norm_tile(t, carry):
        cols = pl.ds(pl.multiple_of(t * 512, 512), 512)
        values = xg[:, :, cols].reshape(4 * rows, 512).astype(f32)
        values = (values - all_mean) * all_scale
        nx[:, cols] = pltpu.roll(values, 4 * rows - (rows - 1), 0).astype(bf16)
        return carry

    lax.fori_loop(0, width // 512, norm_tile, 0)

    loads[0].wait()

    def query_tile(t, carry):
        cols = pl.ds(pl.multiple_of(t * 512, 512), 512)
        qp[:, :, cols] = dot(nx[...], wq[:, cols]).astype(bf16).reshape(4, rows, 512)
        return carry

    lax.fori_loop(0, wq.shape[1] // 512, query_tile, 0)
    copies = [
        go(db_copy(qp.at[db_at(k)], qr.at[me], qp_s.at[k - 1], qp_r.at[k - 1], k)) for k in (1, 2, 3)
    ]
    for copy in copies:
        copy.wait_recv()
    total = qp[me].astype(f32)
    for k in (1, 2, 3):
        total = total + qr[db_at(k)].astype(f32)
    qg[me] = total.astype(bf16)
    copies = [go(db_copy(qg.at[me], qg.at[me], qg_s.at[k - 1], qg_r.at[k - 1], k)) for k in (1, 2, 3)]
    loads[2].wait()
    for copy in copies:
        copy.wait_recv()

    def spot(a, n):
        return place[near[a, n]]

    def owner(a, n):
        return lax.div(spot(a, n), store)

    odd = jnp.where((owner(1, 0) == me) | (owner(1, 1) == me), 1, 0)
    lane = lax.broadcasted_iota(jnp.int32, (rows, 128), 1)
    logs = jnp.zeros((rows, 128), f32)
    for r in range(2):
        span = 2 * r + odd
        which = jnp.where(owner(span, 1) == me, 1, 0)
        slot = lax.rem(spot(span, which), store)
        for h in range(heads):
            cols = slice(h * HDIM, (h + 1) * HDIM)
            scores = lax.dot_general(
                qg[span, :, cols], kvs[slot, 0, :, cols], (((1,), (1,)), ((), ())),
                preferred_element_type=f32,
            ) * HDIM ** (-0.5)
            top = jnp.max(scores, axis=1, keepdims=True)
            raised = jnp.exp(scores - top)
            norm = jnp.sum(raised, axis=1, keepdims=True)
            ob[me, r, :, cols] = dot(
                (raised / norm).astype(bf16), kvs[slot, 1, :, cols]
            ).astype(bf16)
            logs = jnp.where(lane == r * heads + h, top + jnp.log(norm), logs)
    lse[me] = logs
    copies = []
    for k in (1, 2, 3):
        copies.append(go(db_copy(lse.at[me], lse.at[me], ls_s.at[k - 1], ls_r.at[k - 1], k)))
        copies.append(go(db_copy(ob.at[me], ob.at[me], ob_s.at[k - 1], ob_r.at[k - 1], k)))
    loads[1].wait()
    for copy in copies:
        copy.wait_recv()
    for a in range(4):
        r = a // 2
        first, second = owner(a, 0), owner(a, 1)
        log_a, log_b = lse[first], lse[second]
        for h in range(heads):
            cols = slice(h * HDIM, (h + 1) * HDIM)
            at = r * heads + h
            gap = log_b[:, at:at + 1] - log_a[:, at:at + 1]
            mixed = ob[first, r, :, cols].astype(f32) / (1.0 + jnp.exp(gap)) + ob[
                second, r, :, cols
            ].astype(f32) / (1.0 + jnp.exp(-gap))
            att[a * rows:(a + 1) * rows, cols] = mixed.astype(bf16)

    def out_tile(t, carry):
        cols = pl.ds(pl.multiple_of(t * 512, 512), 512)
        part = pltpu.roll(dot(att[...], wd[pl.ds(0, 1024), cols]), rows - 1, 0)
        row_id = lax.broadcasted_iota(jnp.int32, part.shape, 0)
        part = jnp.where(row_id < rows - 1, 0.0, part)
        op[:, :, cols] = part.astype(bf16).reshape(4, rows, 512)
        return carry

    lax.fori_loop(0, width // 512, out_tile, 0)
    total = act[...].astype(f32) + reduce_to_owner(op, orx, op_s, op_r)
    first_down = pltpu.make_async_copy(
        wd_hbm.at[pl.ds(0, 1024)], wd.at[pl.ds(0, 1024)], wd0_sem
    )
    first_down.start()
    state[...] = total
    st_mid[me] = row_sums(total)
    copies = [go(db_copy(st_mid.at[me], st_mid.at[me], sm_s.at[k - 1], sm_r.at[k - 1], k)) for k in (1, 2, 3)]
    for copy in copies:
        copy.wait_recv()
    row_mean, row_scale = mean_and_scale(st_mid[0] + st_mid[1] + st_mid[2] + st_mid[3])
    ng[hs] = ((state[...] - row_mean) * row_scale).astype(bf16)
    finish = spread(ng.at[hs], ng, ng_s, ng_r)
    loads[3].wait()

    finish()

    pieces, wide = lp.shape[1], lp.shape[3]
    half = 2 * rows
    first_down.wait()
    for load in loads[4:]:
        load.wait()
    acc[...] = jnp.zeros_like(acc)
    lines = ((me, lax.rem(me + 1, 4), lax.rem(me + 3, 4)), (3 - me, lax.rem(me + 3, 4), lax.rem(me + 1, 4)))

    def along(src, dst, send, recv, peer):
        return pltpu.make_async_remote_copy(
            src_ref=src, dst_ref=dst, send_sem=send, recv_sem=recv,
            device_id={"db": peer}, device_id_type=pl.DeviceIdType.MESH,
        )

    def sum_copy(way, c, src):
        return along(
            src.at[way, c], lr.at[way, c], lp_s.at[way, c], lp_r.at[way, c], lines[way][1]
        )

    def back_copy(way, c):
        return along(
            ag.at[way, c], ag.at[way, c], ag_s.at[way, c], ag_r.at[way, c], lines[way][2]
        )

    def step(t, carry):
        @pl.when(t < pieces)
        def _():
            cols = pl.ds(pl.multiple_of(t * wide, wide), wide)
            part = dot(ng[...].reshape(4 * rows, width), wu[:, cols])
            lp[:, t] = part.astype(bf16).reshape(2, half, wide)
            for way in range(2):

                @pl.when(lines[way][0] == 0)
                def _():
                    sum_copy(way, t, lp).start()

        for way in range(2):
            spot_on = lines[way][0]
            c = t - (2 * spot_on - 1)

            @pl.when((spot_on > 0) & (c >= 0) & (c < pieces))
            def _():
                sum_copy(way, c, lr).wait_recv()
                total = lr[way, c].astype(f32) + lp[way, c].astype(f32)

                @pl.when(spot_on < 3)
                def _():
                    lr[way, c] = total.astype(bf16)
                    sum_copy(way, c, lr).start()

                @pl.when(spot_on == 3)
                def _():
                    ag[way, c] = jax.nn.gelu(total, approximate=True).astype(bf16)
                    back_copy(way, c).start()

        for way in range(2):
            spot_on = lines[way][0]
            c = t - 14 + 3 * spot_on

            @pl.when((c >= 0) & (c < pieces))
            def _():
                @pl.when(spot_on < 3)
                def _():
                    back_copy(way, c).wait_recv()

                    @pl.when(spot_on > 0)
                    def _():
                        back_copy(way, c).start()

                @pl.when(lax.rem(c, 2) == 1)
                def _():
                    deep = pl.ds(pl.multiple_of((c - 1) * wide, 2 * wide), 2 * wide)
                    left = jnp.concatenate([ag[way, c - 1], ag[way, c]], axis=1)
                    for n in range(width // 512):
                        cols = slice(n * 512, (n + 1) * 512)
                        acc[way * half:(way + 1) * half, cols] += dot(left, wd[deep, cols])

        return carry

    lax.fori_loop(0, pieces + 14, step, 0)
    dp[...] = acc[...].astype(bf16).reshape(dp.shape)
    total = reduce_to_owner(dp, dr, dp_s, dp_r)
    out[...] = (state[...] + total).astype(bf16)

    def drain(c, carry):
        for way in range(2):

            @pl.when(lines[way][0] < 3)
            def _():
                sum_copy(way, c, lr).wait_send()

            @pl.when(lines[way][0] > 0)
            def _():
                back_copy(way, c).wait_send()

        return carry

    lax.fori_loop(0, pieces, drain, 0)
    for copy in sends:
        copy.wait_send()


def fused(activations, w_query, w_out, w_up, w_down, kv_store, neighbours, block_place):
    f32, bf16 = jnp.float32, jnp.bfloat16
    rows, width = activations.shape
    qw = w_query.shape[1]
    hidden = w_up.shape[1]
    vmem = pl.BlockSpec(memory_space=pltpu.VMEM)
    smem = pl.BlockSpec(memory_space=pltpu.SMEM)
    hbm = pl.BlockSpec(memory_space=pl.ANY)
    wide = hidden // PIECES
    scratch = [
        pltpu.VMEM(w_query.shape, bf16),
        pltpu.VMEM(w_up.shape, bf16),
        pltpu.VMEM((hidden, width), bf16),
        pltpu.VMEM(kv_store.shape, bf16),
        pltpu.VMEM((4, rows, width), bf16),
        pltpu.VMEM((4, rows, 256), f32),
        pltpu.VMEM((4, rows, 256), f32),
        pltpu.VMEM((4 * rows, width), bf16),
        pltpu.VMEM((4, rows, qw), bf16),
        pltpu.VMEM((4, rows, qw), bf16),
        pltpu.VMEM((4, rows, qw), bf16),
        pltpu.VMEM((4, 2, rows, qw), bf16),
        pltpu.VMEM((4, rows, 128), f32),
        pltpu.VMEM((4 * rows, qw), bf16),
        pltpu.VMEM((4, rows, width), bf16),
        pltpu.VMEM((3, rows, width), bf16),
        pltpu.VMEM((rows, width), f32),
        pltpu.VMEM((4, rows, 256), f32),
        pltpu.VMEM((4, rows, width), bf16),
        pltpu.VMEM((2, PIECES, 2 * rows, wide), bf16),
        pltpu.VMEM((2, PIECES, 2 * rows, wide), bf16),
        pltpu.VMEM((2, PIECES, 2 * rows, wide), bf16),
        pltpu.VMEM((4 * rows, width), f32),
        pltpu.VMEM((4, rows, width), bf16),
        pltpu.VMEM((3, rows, width), bf16),
        pltpu.SemaphoreType.DMA((7,)),
        pltpu.SemaphoreType.DMA,
    ]
    scratch += [pltpu.SemaphoreType.DMA((3,)) for _ in range(22)]
    scratch += [pltpu.SemaphoreType.DMA((2, PIECES)) for _ in range(4)]
    return pl.pallas_call(
        layer_kernel,
        out_shape=jax.ShapeDtypeStruct((rows, width), bf16),
        in_specs=[vmem, hbm, hbm, hbm, hbm, hbm, smem, smem],
        out_specs=vmem,
        scratch_shapes=scratch,
        compiler_params=pltpu.CompilerParams(
            collective_id=0, has_side_effects=True, vmem_limit_bytes=VMEM_BYTES
        ),
    )(activations, w_query, w_out, w_up, w_down, kv_store, neighbours, block_place)


def solution(mesh):
    in_specs = (
        P(("grp", "head", "sub"), "db"),
        P("db", ("head", "sub")),
        P(("head", "sub"), "db"),
        P("db", ("head", "sub")),
        P(("head", "sub"), "db"),
        P(("grp", "db"), None, None, ("head", "sub")),
        P("grp", None),
        P("grp"),
    )
    out_specs = P(("grp", "head", "sub"), "db")
    sizes = mesh.shape
    body = fused if (sizes["db"], sizes["head"], sizes["sub"]) == (4, 2, 2) else local
    return jax.shard_map(body, mesh=mesh, in_specs=in_specs, out_specs=out_specs, check_vma=False)
```
